128 devices in a mesh: gx: 32 (over x, z, core), gy: 4 (over y).
Axes of the slice: x: 4, y: 4, z: 4, core: 2. Of those that a mesh axis runs over, the one named last changes fastest.
Arguments:
- tracers: float32 [2, 16, 32, 2048], P(None, None, 'gy', 'gx'), may hold values from -6 to 6
- u_face: float32 [16, 32, 2048], P(None, 'gy', 'gx'), may hold values from -0.45 to 0.45
- v_face: float32 [16, 32, 2048], P(None, 'gy', 'gx'), may hold values from -0.45 to 0.45
- thickness: float32 [16, 32, 2048], P(None, 'gy', 'gx'), may hold values from 0.5 to 2
- land_mask: int32 [32, 2048], P('gy', 'gx'), may hold values 0 or 1
- counts: int32 [128, 128], P(('gx', 'gy')), may hold values from 64 to 256, as said below
- ocean_cell: int32 [128, 128, 256], P(('gx', 'gy')), may hold values from 0 to 511
- xgrid_weight: float32 [128, 128, 256], P(('gx', 'gy')), may hold values from 0.05 to 1
- atm_cell: int32 [128, 128, 256], P(('gx', 'gy')), may hold values from 0 to 6911
Outputs:
- tracers_new: float32 [2, 16, 32, 2048], P(None, None, 'gy', 'gx')
- atm_flux: float32 [4, 884736], P(None, ('gx', 'gy'))
The draws below stay inside these ranges and needn't reach their ends.
Inputs may be any that keep to these rules, and one draw needn't show every extreme that they name: Slots k >= counts[s, o] carry no intersection. One owner, drawn per input, has all 256 slots used from every sender. `ocean_cell`: indexes the sender's tile row-major over 8 x 64 cells; read only in used slots. `atm_cell`: indexes the owner's 6912 cells; slot (s, o, k) here belongs to slot (s, o, k) of ocean_cell.
All inputs are finite; a program needn't handle non-finite values. No bound on the sum of `land_mask` on one device may be relied on, other than what follows from the above.
Results may differ from the reference program's by a relative error of at most 0.0003.
Values sent between devices are 32-bit elements; how exact they have to be, the bound alone decides.
No kernel may reach another device: no remote copies, remote signals or barrier semaphores. Data moves between devices by JAX's collectives and lax.ppermute only.
A program may use at most 64 MiB of HBM per device.

```python
import math
import jax
import jax.numpy as jnp
from jax import lax

CLAT = 8
CLON = 64
LEV = 16
A_DEV = 6912
CAP = 256
NLAT = 32
NLON = 2048
ATM = 884736
N_GY = 4
DEVICES = 128


def draw_counts(key, part):
    ceiling_key, count_key, full_key = jax.random.split(jax.random.fold_in(key, 17), 3)
    ceiling = jax.random.randint(ceiling_key, (DEVICES,), CAP // 2, CAP + 1)
    lower = ceiling // 2
    drawn_counts = jax.random.randint(count_key, (DEVICES, DEVICES), lower[None, :], ceiling[None, :] + 1)
    chosen_owner = jax.random.randint(full_key, (), 0, DEVICES)
    owner_ids = lax.broadcasted_iota(jnp.int32, (DEVICES, DEVICES), 1)
    return jnp.where(owner_ids == chosen_owner, CAP, drawn_counts).astype(jnp.int32)


def touch_ends(result, stream_key, smallest, largest):
    extent = result.shape
    place = [jax.random.randint(jax.random.fold_in(stream_key, axis), (), 0, extent[axis]) for axis in range(len(extent))]
    result = result.at[tuple(place)].set(smallest)
    longest = extent.index(max(extent))
    place[longest] = (place[longest] + 1) % extent[longest]
    return result.at[tuple(place)].set(largest)


def steps_of(rng, dims, cuts, smallest, largest):
    level = 1.0
    for dim, shards_of in cuts:
        heights = jax.random.uniform(jax.random.fold_in(jax.random.fold_in(rng, 6), dim), (shards_of,), jnp.float32, smallest / len(cuts), largest / len(cuts))
        level = level * jnp.repeat(jnp.exp(heights), dims[dim] // shards_of).reshape((-1,) + (1,) * (len(dims) - 1 - dim))
    return level


def centred(key, shape, width, bound, pieces=(), held_as=jnp.bfloat16):
    gain = steps_of(key, shape, pieces, -0.22, 0.18) if pieces else 1.0
    values = jax.random.normal(key, shape, jnp.float32) * width * gain
    return jnp.minimum(jnp.maximum(values, -bound), bound).astype(held_as)


def setup_inputs(seed: int = 0) -> dict:
    key_of = jax.random.split(jax.random.key(seed), 10)
    tracers = centred(key_of[0], (2, LEV, NLAT, NLON), 1.0, 6.0, ((2, 4), (3, 32)), jnp.float32)
    u_face = jnp.clip(jax.random.uniform(key_of[1], (LEV, NLAT, NLON), jnp.float32, -0.45, 0.45) * steps_of(key_of[1], (LEV, NLAT, NLON), ((1, 4), (2, 32)), -0.4, 0.0), -0.45, 0.45)
    v_face = jnp.clip(jax.random.uniform(key_of[2], (LEV, NLAT, NLON), jnp.float32, -0.45, 0.45) * steps_of(key_of[2], (LEV, NLAT, NLON), ((1, 4), (2, 32)), -0.4, 0.0), -0.45, 0.45)
    thickness = jnp.clip(jnp.exp(math.log(2.0) - 1.3862944 * jax.random.uniform(key_of[3], (LEV, NLAT, NLON), jnp.float32) ** steps_of(key_of[3], (LEV, NLAT, NLON), ((1, 4), (2, 32)), -0.2, 0.2)), 0.5, 2.0)
    land_mask = touch_ends((jax.random.randint(key_of[4], (NLAT, NLON), 0, 10) < 7).astype(jnp.int32), jax.random.fold_in(key_of[4], 1), 0, 1)
    counts = draw_counts(jax.random.fold_in(key_of[9], 71), 0)
    ocean_cell = touch_ends(jax.random.randint(key_of[6], (DEVICES, DEVICES, CAP), 0, CLAT * CLON), jax.random.fold_in(key_of[6], 1), 0, (CLAT * CLON) - 1).astype(jnp.int32)
    xgrid_weight = jnp.clip(jnp.exp(math.log(1.0) - 2.9957323 * jax.random.uniform(key_of[7], (DEVICES, DEVICES, CAP), jnp.float32) ** steps_of(key_of[7], (DEVICES, DEVICES, CAP), ((0, 128),), -0.2, 0.2)), 0.05, 1.0)
    atm_cell = touch_ends(jax.random.randint(key_of[8], (DEVICES, DEVICES, CAP), 0, A_DEV), jax.random.fold_in(key_of[8], 1), 0, A_DEV - 1).astype(jnp.int32)
    return {"tracers": tracers, "u_face": u_face, "v_face": v_face, "thickness": thickness, "land_mask": land_mask, "counts": counts, "ocean_cell": ocean_cell, "xgrid_weight": xgrid_weight, "atm_cell": atm_cell}


def window_cut(values, lead_cut, tail_cut, sweep_axis):
    return lax.slice_in_dim(values, lead_cut, values.shape[sweep_axis] - tail_cut, axis=sweep_axis)

def ppm_sweep(padded, velocity, wet_cells, sweep_axis):
    edge_values = (7.0 * (window_cut(padded, 1, 2, sweep_axis) + window_cut(padded, 2, 1, sweep_axis)) - (window_cut(padded, 0, 3, sweep_axis) + window_cut(padded, 3, 0, sweep_axis))) / 12.0
    left_edge = window_cut(edge_values, 0, 1, sweep_axis)
    right_edge = window_cut(edge_values, 1, 0, sweep_axis)
    centre_vals = window_cut(padded, 2, 2, sweep_axis)
    slope_diff = right_edge - left_edge
    curvature = 6.0 * centre_vals - 3.0 * (left_edge + right_edge)
    courant = window_cut(velocity, 2, 3, sweep_axis) * window_cut(wet_cells, 2, 3, sweep_axis) * window_cut(wet_cells, 3, 2, sweep_axis)
    backward = -courant
    up_flux = courant * (window_cut(right_edge, 0, 1, sweep_axis) - 0.5 * courant * (window_cut(slope_diff, 0, 1, sweep_axis) - (1.0 - courant * (2.0 / 3.0)) * window_cut(curvature, 0, 1, sweep_axis)))
    down_flux = courant * (window_cut(left_edge, 1, 0, sweep_axis) + 0.5 * backward * (window_cut(slope_diff, 1, 0, sweep_axis) + (1.0 - backward * (2.0 / 3.0)) * window_cut(curvature, 1, 0, sweep_axis)))
    flux_face = jnp.where(courant >= 0.0, up_flux, down_flux)
    return window_cut(padded, 3, 3, sweep_axis) - (window_cut(flux_face, 1, 0, sweep_axis) - window_cut(flux_face, 0, 1, sweep_axis))

def vertical_remap(fields, thickness):
    levels = thickness.shape[0]
    bottoms = jnp.cumsum(thickness, axis=0)
    starts = jnp.concatenate([jnp.zeros_like(bottoms[:1]), bottoms[:-1]], axis=0)
    target_thick = bottoms[-1] / levels
    results = []
    for target_level in range(levels):
        layer_top = target_thick * target_level
        layer_base = target_thick * (target_level + 1)
        shared_depth = jnp.maximum(jnp.minimum(bottoms, layer_base) - jnp.maximum(starts, layer_top), 0.0)
        results.append(lax.optimization_barrier(jnp.sum(shared_depth[None] * fields, axis=1)) / target_thick)
    return jnp.stack(results, axis=1)

def surface_fields(tracers, u_face, v_face):
    east_current = u_face[0]
    north_current = v_face[0]
    surface_speed = jnp.sqrt(east_current * east_current + north_current * north_current + 0.01)
    return jnp.stack([tracers[0, 0] * surface_speed, tracers[1, 0] * surface_speed, east_current * surface_speed, north_current * surface_speed]).reshape(4, -1)

def pad_global(values):
    lead_dims = [(0, 0)] * (values.ndim - 2)
    return jnp.pad(values, lead_dims + [(3, 3), (3, 3)])

def reference(tracers, u_face, v_face, thickness, land_mask, counts, ocean_cell, xgrid_weight, atm_cell):
    wet_cells = land_mask.astype(jnp.float32)
    wet_pad = pad_global(wet_cells)[None, None]

    def advect_level(inputs):
        level_fields, east_vel, north_vel = inputs
        field_pad = pad_global(level_fields[:, None])
        east_pad = pad_global(east_vel)[None, None]
        north_pad = pad_global(north_vel)[None, None]
        x_swept = ppm_sweep(field_pad, east_pad, wet_pad, 3)
        y_swept = ppm_sweep(x_swept, north_pad[..., 3:-3], wet_pad[..., 3:-3], 2)
        return y_swept[:, 0]
    advected = lax.map(advect_level, (jnp.moveaxis(tracers, 1, 0), u_face, v_face))
    advected = jnp.moveaxis(advected, 0, 1)
    tracers_new = vertical_remap(advected, thickness)
    fields = surface_fields(tracers, u_face, v_face)
    sender_ids = lax.broadcasted_iota(jnp.int32, (DEVICES, DEVICES, CAP), 0)
    owner_ids = lax.broadcasted_iota(jnp.int32, (DEVICES, DEVICES, CAP), 1)
    slot_ids = lax.broadcasted_iota(jnp.int32, (DEVICES, DEVICES, CAP), 2)
    lat_index = sender_ids % N_GY * CLAT + ocean_cell // CLON
    lon_index = sender_ids // N_GY * CLON + ocean_cell % CLON
    flat_index = (lat_index * NLON + lon_index).reshape(-1)
    slot_used = (slot_ids < counts[:, :, None]).astype(jnp.float32).reshape(-1)
    row_share = xgrid_weight.reshape(-1) * wet_cells.reshape(-1)[flat_index] * slot_used
    picked = fields[:, flat_index] * row_share[None]
    contributions = jnp.concatenate([picked, row_share[None]], axis=0)
    targets = (owner_ids * A_DEV + jnp.swapaxes(atm_cell, 0, 1)).reshape(-1)
    totals = jnp.zeros((5, ATM), jnp.float32).at[:, targets].add(contributions)
    atm_flux = totals[:4] / jnp.maximum(totals[4:5], 0.2)
    return (tracers_new, atm_flux)
```

```python
import jax
import jax.numpy as jnp
from jax import lax
from jax.experimental import pallas as pl
from jax.experimental.pallas import tpu as pltpu
from jax.sharding import PartitionSpec as P

A_DEV = 6912
def lane_take(table, lanes):
    return jnp.take_along_axis(table, lanes, axis=1, mode="promise_in_bounds")

def gather_kernel(tracers, u_face, v_face, land_mask, counts, ocean_cell, weight, payload):
    def packed(x):
        return jnp.concatenate([x[0:4, :], x[4:8, :]], axis=1)
    wet = packed(land_mask[...].astype(jnp.float32))
    east = packed(u_face[0]); north = packed(v_face[0])
    speed = jnp.sqrt(east * east + north * north + 0.01) * wet
    fields = [packed(tracers[0, 0]) * speed, packed(tracers[1, 0]) * speed, east * speed, north * speed, wet]
    tables = [[jnp.broadcast_to(f[q:q+1, :], (8, 128)) for q in range(4)] for f in fields]
    used = jnp.broadcast_to(counts[...], (8, 128))
    sub = lax.broadcasted_iota(jnp.int32, (8, 128), 0)
    lane_ids = lax.broadcasted_iota(jnp.int32, (8, 128), 1)
    def step(g, _):
        o = pl.multiple_of(g * 8, 8)
        count = lane_take(used, sub + o)
        for h in range(2):
            cell = ocean_cell[0, pl.ds(o, 8), h*128:(h+1)*128]
            share = jnp.where(lane_ids + h*128 < count, weight[0, pl.ds(o, 8), h*128:(h+1)*128], 0.0)
            lanes = (cell & 63) | ((cell >> 2) & 64)
            odd = (cell & 64) != 0
            upper = (cell & 128) != 0
            for f in range(5):
                a, b, c, d = [lane_take(t, lanes) for t in tables[f]]
                val = jnp.where(upper, jnp.where(odd, d, c), jnp.where(odd, b, a))
                payload[pl.ds(g * 80 + f*2+h, 8, stride=10), :] = val * share
        return 0
    lax.fori_loop(0, 16, step, 0, unroll=2)

def gather(tracers, u_face, v_face, land_mask, counts, ocean_cell, weight):
    return pl.pallas_call(gather_kernel, grid=(1,),
      in_specs=[pl.BlockSpec((2,1,8,64), lambda i:(0,0,0,0)), pl.BlockSpec((1,8,64), lambda i:(0,0,0)), pl.BlockSpec((1,8,64), lambda i:(0,0,0)),
        pl.BlockSpec((8,64), lambda i:(0,0)), pl.BlockSpec((1,128), lambda i:(0,0)), pl.BlockSpec((1,128,256), lambda i:(0,0,0)), pl.BlockSpec((1,128,256), lambda i:(0,0,0))],
      out_specs=pl.BlockSpec((1280,128), lambda i:(0,0)),
      out_shape=jax.ShapeDtypeStruct((1280,128), jnp.float32),
      name="gather_rows")(tracers, u_face, v_face, land_mask, counts, ocean_cell, weight)

def scatter_kernel(received, atm_cell, flux, rows_a, rows_b, acc, fin):
    iota16 = lax.broadcasted_iota(jnp.int32, (16, 128), 0).astype(jnp.bfloat16)
    zero = jnp.zeros((16,128), jnp.bfloat16); one = jnp.ones((16,128), jnp.bfloat16)
    def bc(row):
        return jnp.broadcast_to(row, (16, 128)).astype(jnp.bfloat16)
    def build(g, slot):
        s0 = pl.multiple_of(g * 8, 8)
        for h in range(2):
            cell = atm_cell[0, pl.ds(s0, 8), h*128:(h+1)*128]
            high = (cell >> 8).astype(jnp.float32)
            low = (cell & 255).astype(jnp.float32)
            pieces = []
            for f in range(5):
                val = received[pl.ds(g * 80 + f*2+h, 8, stride=10), :]
                top = val.astype(jnp.bfloat16).astype(jnp.float32)
                pieces += [top, val - top]
            for s in range(8):
                cols = slice((s*2+h)*128, (s*2+h+1)*128)
                lo = bc(low[s:s+1, :])
                for k in range(16):
                    rows_b[slot, k*16:(k+1)*16, cols] = jnp.where(lo == iota16 + jnp.bfloat16(k*16), one, zero)
                hi = bc(high[s:s+1, :])
                m = [hi == iota16, hi == iota16 + jnp.bfloat16(16)]
                for j in range(10):
                    p = bc(pieces[j][s:s+1, :])
                    for k in range(2):
                        rows_a[slot, (j*2+k)*16:(j*2+k+1)*16, cols] = jnp.where(m[k], p, zero)
    def mult(slot):
        acc[...] += lax.dot_general(rows_a[slot], rows_b[slot], (((1,),(1,)),((),())), preferred_element_type=jnp.float32)
    acc[...] = jnp.zeros_like(acc)
    build(0, 0)
    def step(i, _):
        build(2*i+1, 1)
        mult(0)
        build(jnp.minimum(2*i+2, 15), 0)
        mult(1)
        return 0
    lax.fori_loop(0, 8, step, 0)
    for half in range(2):
        for f in range(5):
            fin[half*160+f*32:half*160+f*32+32, :] = acc[f*64:f*64+32, half*128:half*128+128] + acc[f*64+32:f*64+64, half*128:half*128+128]
    for hi in range(27):
        for half in range(2):
            num = fin[pl.ds(half*160+hi, 4, stride=32), :]
            den = fin[half*160+128+hi:half*160+129+hi, :]
            flux[:, hi*256+half*128:hi*256+half*128+128] = num / jnp.maximum(den, 0.2)

def scatter(received, atm_cell):
    return pl.pallas_call(scatter_kernel,
      in_specs=[pl.BlockSpec(memory_space=pltpu.VMEM)]*2,
      out_specs=pl.BlockSpec(memory_space=pltpu.VMEM),
      out_shape=jax.ShapeDtypeStruct((4,A_DEV), jnp.float32),
      scratch_shapes=[pltpu.VMEM((2,320,2048), jnp.bfloat16), pltpu.VMEM((2,256,2048), jnp.bfloat16), pltpu.VMEM((320,256), jnp.float32), pltpu.VMEM((320,128), jnp.float32)],
      compiler_params=pltpu.CompilerParams(vmem_limit_bytes=40*2**20),
      name="scatter_add")(received, atm_cell)


def extended(array, sides, width):
    for axis, dim in sides:
        size, length = (lax.axis_size(axis), array.shape[dim])
        up = [(i, (i + 1) % size) for i in range(size - 1)]
        down = [(j, i) for i, j in up]
        last = lax.slice_in_dim(array, length - width, length, axis=dim)
        first = lax.slice_in_dim(array, 0, width, axis=dim)
        before = lax.ppermute(last, axis, up)
        after = lax.ppermute(first, axis, down)
        array = jnp.concatenate([before, array, after], axis=dim)
    return array


def window_cut(values, lead_cut, tail_cut, sweep_axis):
    return lax.slice_in_dim(values, lead_cut, values.shape[sweep_axis] - tail_cut, axis=sweep_axis)


def ppm_sweep(padded, velocity, wet_cells, sweep_axis):
    edge_values = (
        7.0 * (window_cut(padded, 1, 2, sweep_axis) + window_cut(padded, 2, 1, sweep_axis))
        - (window_cut(padded, 0, 3, sweep_axis) + window_cut(padded, 3, 0, sweep_axis))
    ) / 12.0
    left_edge = window_cut(edge_values, 0, 1, sweep_axis)
    right_edge = window_cut(edge_values, 1, 0, sweep_axis)
    centre_vals = window_cut(padded, 2, 2, sweep_axis)
    slope_diff = right_edge - left_edge
    curvature = 6.0 * centre_vals - 3.0 * (left_edge + right_edge)
    courant = (
        window_cut(velocity, 2, 3, sweep_axis)
        * window_cut(wet_cells, 2, 3, sweep_axis)
        * window_cut(wet_cells, 3, 2, sweep_axis)
    )
    backward = -courant
    up_flux = courant * (
        window_cut(right_edge, 0, 1, sweep_axis)
        - 0.5
        * courant
        * (
            window_cut(slope_diff, 0, 1, sweep_axis)
            - (1.0 - courant * (2.0 / 3.0)) * window_cut(curvature, 0, 1, sweep_axis)
        )
    )
    down_flux = courant * (
        window_cut(left_edge, 1, 0, sweep_axis)
        + 0.5
        * backward
        * (
            window_cut(slope_diff, 1, 0, sweep_axis)
            + (1.0 - backward * (2.0 / 3.0)) * window_cut(curvature, 1, 0, sweep_axis)
        )
    )
    flux_face = jnp.where(courant >= 0.0, up_flux, down_flux)
    return window_cut(padded, 3, 3, sweep_axis) - (
        window_cut(flux_face, 1, 0, sweep_axis) - window_cut(flux_face, 0, 1, sweep_axis)
    )


def vertical_remap(fields, thickness):
    levels = thickness.shape[0]
    bottoms = jnp.cumsum(thickness, axis=0)
    starts = jnp.concatenate([jnp.zeros_like(bottoms[:1]), bottoms[:-1]], axis=0)
    target_thick = bottoms[-1] / levels
    results = []
    for target_level in range(levels):
        layer_top = target_thick * target_level
        layer_base = target_thick * (target_level + 1)
        shared_depth = jnp.maximum(
            jnp.minimum(bottoms, layer_base) - jnp.maximum(starts, layer_top), 0.0
        )
        results.append(jnp.sum(shared_depth[None] * fields, axis=1) / target_thick)
    return jnp.stack(results, axis=1)


def on_device(
    tracers, u_face, v_face, thickness, land_mask, counts, ocean_cell, xgrid_weight, atm_cell
):
    levels = tracers.shape[1]
    tile_rows = tracers.shape[2]
    tile_cols = tracers.shape[3]
    wet_cells = land_mask.astype(jnp.float32)
    payload = gather(tracers, u_face, v_face, land_mask, counts, ocean_cell, xgrid_weight)
    received = lax.all_to_all(payload.reshape(128, 1, 1280), ("gx", "gy"), split_axis=0, concat_axis=0, tiled=True)
    atm_flux = scatter(received.reshape(1280, 128), atm_cell)
    stacked = jnp.concatenate(
        [tracers.reshape(2 * levels, tile_rows, tile_cols), u_face, v_face, wet_cells[None]], axis=0
    )
    widened = extended(stacked, (("gy", 1),), 3)
    padded = extended(widened, (("gx", 2),), 3)
    field_pad = padded[: 2 * levels].reshape(2, levels, tile_rows + 6, tile_cols + 6)
    east_pad = padded[2 * levels : 3 * levels][None]
    north_pad = padded[3 * levels : 4 * levels][None]
    wet_pad = padded[4 * levels :][None]
    x_swept = ppm_sweep(field_pad, east_pad, wet_pad, 3)
    advected = ppm_sweep(x_swept, north_pad[..., 3:-3], wet_pad[..., 3:-3], 2)
    tracers_new = vertical_remap(advected, thickness)
    return (tracers_new, atm_flux)


def solution(mesh):
    placed = (
        P(None, None, "gy", "gx"),
        P(None, "gy", "gx"),
        P(None, "gy", "gx"),
        P(None, "gy", "gx"),
        P("gy", "gx"),
        P(("gx", "gy"), None),
        P(("gx", "gy"), None, None),
        P(("gx", "gy"), None, None),
        P(("gx", "gy"), None, None),
    )
    return jax.shard_map(
        on_device,
        mesh=mesh,
        in_specs=placed,
        out_specs=(P(None, None, "gy", "gx"), P(None, ("gx", "gy"))),
        check_vma=False,
    )
```

```python
import functools

import jax
import jax.numpy as jnp
from jax import lax
from jax.experimental import pallas as pl
from jax.experimental.pallas import tpu as pltpu
from jax.sharding import PartitionSpec as P

A_DEV = 6912
HI = 27
PER = 4

def lanes_of(shape):
    return lax.broadcasted_iota(jnp.int32, shape, len(shape) - 1)

def wide(x, y=None):
    return jnp.concatenate([x, x if y is None else y], axis=1)

def strips_kernel(tracers, u_face, land_mask, to_east, to_west):
    lane = lanes_of((8, 128))
    spot = lane & 3
    east = jnp.zeros((8, 128), jnp.float32)
    west = jnp.zeros((8, 128), jnp.float32)
    wet = wide(land_mask[...].astype(jnp.float32))
    for p in range(32):
        here = lane >> 2 == p
        cells = wide(tracers[p // 16, p % 16])
        east = jnp.where(here, pltpu.roll(cells, (4 * p - 61) % 128, 1), east)
        west = jnp.where(here, pltpu.roll(cells, 4 * p, 1), west)
        last = 4 * p + 3
        if p < 16:
            east = jnp.where(lane == last, pltpu.roll(wide(u_face[p]), (last - 63) % 128, 1), east)
        elif p == 16:
            east = jnp.where(lane == last, pltpu.roll(wet, (last - 63) % 128, 1), east)
            west = jnp.where(lane == last, pltpu.roll(wet, last, 1), west)
    to_east[...] = east
    to_west[...] = west

def sweep(q, c, size, axis):
    def at(x, s):
        return pltpu.roll(x, (-s) % size, axis)
    nxt = at(q, 1)
    edge = (7.0 * (q + nxt) - (at(q, -1) + at(nxt, 1))) * (1.0 / 12.0)
    left = at(edge, -1)
    slope = edge - left
    curve = 6.0 * q - 3.0 * (left + edge)
    east = c >= 0.0
    size_c = jnp.abs(c)
    first = jnp.where(east, -slope, at(slope, 1))
    second = jnp.where(east, curve, at(curve, 1))
    flux = c * (edge + (0.5 * size_c) * (first + (1.0 - size_c * (2.0 / 3.0)) * second))
    return q - (flux - at(flux, -1))

def east_kernel(tracers, u_face, v_face, land_mask, from_west, from_east, swept, to_next, to_prev):
    lane = lanes_of((8, 128))
    own = lane < 64
    west_part = lane >= 96
    west = from_west[...]
    east = from_east[...]
    def put(cells, src, at_lane, lane_here, base):
        return jnp.where(lane == lane_here, pltpu.roll(src, (lane_here - at_lane) % 128, 1), base)
    wet = wide(land_mask[...].astype(jnp.float32))
    wet_x = put(None, west, 67, 127, put(None, east, 67, 64, wet))
    mm = wet_x * pltpu.roll(wet_x, 127, 1)
    for k in range(16):
        u = put(None, west, 4 * k + 3, 127, wide(u_face[k]))
        c = u * mm
        both = []
        for t in range(2):
            p = t * 16 + k
            halo = jnp.where(west_part, pltpu.roll(west, (125 - 4 * p) % 128, 1), pltpu.roll(east, (64 - 4 * p) % 128, 1))
            q = jnp.where(own, wide(tracers[t, k]), halo)
            both.append(sweep(q, c, 128, 1)[:, :64])
        z = wide(both[0], both[1])
        swept[k] = z
        to_next[k, 0:3, :] = z[5:8]
        to_prev[k, 0:3, :] = z[0:3]
        to_next[k, 3:4, :] = wide(v_face[k, 7:8, :], wet[7:8, :64])
        to_prev[k, 3:4, :] = wide(v_face[k, 0:1, :], wet[0:1, :64])

def north_kernel(swept, v_face, land_mask, thickness, from_prev, from_next, out):
    row = lax.broadcasted_iota(jnp.int32, (8, 128), 0)
    lane = lanes_of((8, 128))
    wet = wide(land_mask[...].astype(jnp.float32))
    def twin(x):
        return jnp.where(lane < 64, pltpu.roll(x, 64, 1), x)
    def eight(ref, k):
        x = ref[k]
        return jnp.concatenate([x, x], axis=0)
    prev0 = twin(eight(from_prev, 0)); next0 = twin(eight(from_next, 0))
    wet_y = jnp.concatenate([wet, jnp.where(row == 0, pltpu.roll(next0, (0 - 3) % 8, 0), prev0)], axis=0)
    mm = wet_y * pltpu.roll(wet_y, 15, 0)
    def flip(x):
        return jnp.where(lane < 64, x, pltpu.roll(x, 64, 1))
    z = []
    for k in range(16):
        prev = eight(from_prev, k)
        nxt = eight(from_next, k)
        v = jnp.concatenate([wide(v_face[k]), flip(prev)], axis=0)
        q = jnp.concatenate([swept[k], jnp.where(row < 4, nxt, pltpu.roll(prev, 1, 0))], axis=0)
        z.append(sweep(q, v * mm, 16, 0)[:8])
    tops = [jnp.zeros((8, 128), jnp.float32)]
    for j in range(16):
        tops.append(tops[-1] + wide(thickness[j]))
    thick = tops[16] * (1.0 / 16.0)
    inverse = 1.0 / thick
    for k in range(16):
        top = thick * float(k)
        base = thick * float(k + 1)
        total = jnp.zeros((8, 128), jnp.float32)
        for j in range(16):
            depth = jnp.maximum(jnp.minimum(tops[j + 1], base) - jnp.maximum(tops[j], top), 0.0)
            total = total + depth * z[j]
        total = total * inverse
        out[0, k] = total[:, :64]
        out[1, k] = total[:, 64:]

VM = pl.BlockSpec(memory_space=pltpu.VMEM)
def f32(*shape):
    return jax.ShapeDtypeStruct(shape, jnp.float32)
def call(kernel, name, outs, args):
    return pl.pallas_call(kernel, in_specs=[VM] * len(args), out_specs=[VM] * len(outs), out_shape=list(outs), compiler_params=pltpu.CompilerParams(vmem_limit_bytes=8 * 2**20), name=name)(*args)

def shift(x, axis, step):
    n = lax.axis_size(axis)
    pairs = [(i, i + 1) for i in range(n - 1)]
    if step < 0:
        pairs = [(j, i) for i, j in pairs]
    return lax.ppermute(x, axis, pairs)

def advect(tracers, u_face, v_face, thickness, land_mask):
    to_east, to_west = call(strips_kernel, "column_strips", [f32(8, 128)] * 2, (tracers, u_face, land_mask))
    from_west = shift(to_east, "gx", 1)
    from_east = shift(to_west, "gx", -1)
    swept, to_next, to_prev = call(east_kernel, "sweep_longitude", [f32(16, 8, 128), f32(16, 4, 128), f32(16, 4, 128)],
        (tracers, u_face, v_face, land_mask, from_west, from_east))
    from_prev = shift(to_next, "gy", 1)
    from_next = shift(to_prev, "gy", -1)
    return call(north_kernel, "sweep_latitude", [f32(2, 16, 8, 64)], (swept, v_face, land_mask, thickness, from_prev, from_next))[0]


def lane_take(table, lanes):
    return jnp.take_along_axis(table, lanes, axis=1, mode="promise_in_bounds")
def gather_kernel(tracers, u_face, v_face, land_mask, counts, ocean_cell, weight, payload):
    def packed(x):
        return jnp.concatenate([x[0:4, :], x[4:8, :]], axis=1)
    wet = packed(land_mask[...].astype(jnp.float32))
    east = packed(u_face[0]); north = packed(v_face[0])
    speed = jnp.sqrt(east * east + north * north + 0.01) * wet
    fields = [packed(tracers[0, 0]) * speed, packed(tracers[1, 0]) * speed, east * speed, north * speed, wet]
    tables = [[jnp.broadcast_to(f[q:q+1, :], (8, 128)) for q in range(4)] for f in fields]
    used = jnp.broadcast_to(counts[...], (8, 128))
    sub = lax.broadcasted_iota(jnp.int32, (8, 128), 0)
    lane_ids = lax.broadcasted_iota(jnp.int32, (8, 128), 1)
    def step(g, _):
        o = pl.multiple_of(g * 8, 8)
        count = lane_take(used, sub + o)
        for h in range(2):
            cell = ocean_cell[0, pl.ds(o, 8), h*128:(h+1)*128]
            share = jnp.where(lane_ids + h*128 < count, weight[0, pl.ds(o, 8), h*128:(h+1)*128], 0.0)
            lanes = (cell & 63) | ((cell >> 2) & 64)
            odd = (cell & 64) != 0
            upper = (cell & 128) != 0
            for f in range(5):
                a, b, c, d = [lane_take(t, lanes) for t in tables[f]]
                val = jnp.where(upper, jnp.where(odd, d, c), jnp.where(odd, b, a))
                payload[pl.ds(g * 80 + f*2+h, 8, stride=10), :] = val * share
        return 0
    lax.fori_loop(0, 16, step, 0, unroll=16)


def scatter_kernel(received, atm_cell, flux, fin):
    sub = lax.broadcasted_iota(jnp.int32, (16, 128), 0)
    def bf(x):
        return x.astype(jnp.float32).astype(jnp.bfloat16)
    low_ids = [bf(sub + 16 * k) for k in range(16)]
    high_ids = []
    for k in range(17):
        first = (16 * k) // HI
        row = sub + 16 * k - first * HI
        row = jnp.where(row >= HI, row - HI, row)
        if k == 16:
            row = jnp.where(sub < 14, row, -1)
        high_ids.append(bf(row))
    one, zero = jnp.bfloat16(1), jnp.bfloat16(0)
    def spread(row):
        return jnp.broadcast_to(row, (16, 128)).astype(jnp.bfloat16)
    def run(*accs):
        accs = [accs[:17], accs[17:]]
        for m in range(2):
            for a in accs[m]:
                pltpu.matmul_pop(a)
        def chunk(cells, pieces, s, mxu, stage):
            low = [spread((c[s:s+1] & 255).astype(jnp.float32)) for c in cells]
            rhs = jnp.concatenate([jnp.concatenate([jnp.where(lo == ids, one, zero) for lo in low], axis=1) for ids in low_ids], axis=0)
            pltpu.matmul_push_rhs(rhs, stage, mxu, transpose=True)
            high = [spread((c[s:s+1] >> 8).astype(jnp.float32)) for c in cells]
            tiles = {}
            for k in range(17):
                first = (16 * k) // HI
                edge = (first + 1) * HI - 16 * k
                for j in (first, first + 1):
                    if j < 10 and j not in tiles:
                        tiles[j] = [spread(p[s:s+1]) for p in pieces[j]]
                halves = []
                for h in range(2):
                    v = tiles[first][h]
                    if edge < 16 and first + 1 < 10:
                        v = jnp.where(sub < edge, v, tiles[first + 1][h])
                    halves.append(jnp.where(high[h] == high_ids[k], v, zero))
                pltpu.matmul_acc_lhs(accs[mxu][k], jnp.concatenate(halves, axis=1), load_staged_rhs=stage if k == 0 else None)
        def step(i, _):
            for k in range(PER):
                g = i * PER + k
                cells = [atm_cell[0, pl.ds(pl.multiple_of(g * 8, 8), 8), h*128:h*128+128] for h in range(2)]
                pieces = []
                for f in range(5):
                    val = [received[pl.ds(g * 80 + f*2+h, 8, stride=10), :] for h in range(2)]
                    top = [v.astype(jnp.bfloat16).astype(jnp.float32) for v in val]
                    pieces += [top, [v - t for v, t in zip(val, top)]]
                for s in range(8):
                    chunk(cells, pieces, s, s % 2, (s // 2) % 2)
            return 0
        lax.fori_loop(0, 16 // PER, step, 0)
        for k in range(17):
            total = pltpu.matmul_pop(accs[0][k]) + pltpu.matmul_pop(accs[1][k])
            for half in range(2):
                fin[half*272+k*16:half*272+k*16+16, :] = total[:, half*128:half*128+128]
    pl.run_scoped(run, *([pltpu.ACC(0)((16, 256), jnp.float32)] * 17 + [pltpu.ACC(1)((16, 256), jnp.float32)] * 17))
    for hi in range(27):
        for half in range(2):
            b = half * 272 + hi
            num = fin[pl.ds(b, 4, stride=54), :] + fin[pl.ds(b+27, 4, stride=54), :]
            den = fin[b+216:b+217, :] + fin[b+243:b+244, :]
            flux[:, hi*256+half*128:hi*256+half*128+128] = num / jnp.maximum(den, 0.2)


def gather(tracers, u_face, v_face, land_mask, counts, ocean_cell, weight):
    return pl.pallas_call(
        gather_kernel,
        grid=(1,),
        in_specs=[
            pl.BlockSpec((2, 1, 8, 64), lambda i: (0, 0, 0, 0)),
            pl.BlockSpec((1, 8, 64), lambda i: (0, 0, 0)),
            pl.BlockSpec((1, 8, 64), lambda i: (0, 0, 0)),
            pl.BlockSpec((8, 64), lambda i: (0, 0)),
            pl.BlockSpec((1, 128), lambda i: (0, 0)),
            pl.BlockSpec((1, 128, 256), lambda i: (0, 0, 0)),
            pl.BlockSpec((1, 128, 256), lambda i: (0, 0, 0)),
        ],
        out_specs=pl.BlockSpec((1280, 128), lambda i: (0, 0)),
        out_shape=f32(1280, 128),
        name="weighted_slots",
    )(tracers, u_face, v_face, land_mask, counts, ocean_cell, weight)


def scatter(received, atm_cell):
    return pl.pallas_call(
        scatter_kernel,
        in_specs=[VM] * 2,
        out_specs=VM,
        out_shape=f32(4, A_DEV),
        scratch_shapes=[pltpu.VMEM((544, 128), jnp.float32)],
        compiler_params=pltpu.CompilerParams(vmem_limit_bytes=16 * 2**20),
        name="owner_sums",
    )(received, atm_cell)


def on_device(tracers, u_face, v_face, thickness, land_mask, counts, ocean_cell, xgrid_weight, atm_cell):
    payload = gather(tracers, u_face, v_face, land_mask, counts, ocean_cell, xgrid_weight)
    received = lax.all_to_all(payload.reshape(128, 1, 1280), ("gx", "gy"), split_axis=0, concat_axis=0, tiled=True)
    tracers_new = advect(tracers, u_face, v_face, thickness, land_mask)
    atm_flux = scatter(received.reshape(1280, 128), atm_cell)
    return (tracers_new, atm_flux)


def solution(mesh):
    placed = (
        P(None, None, "gy", "gx"),
        P(None, "gy", "gx"),
        P(None, "gy", "gx"),
        P(None, "gy", "gx"),
        P("gy", "gx"),
        P(("gx", "gy"), None),
        P(("gx", "gy"), None, None),
        P(("gx", "gy"), None, None),
        P(("gx", "gy"), None, None),
    )
    return jax.shard_map(
        on_device,
        mesh=mesh,
        in_specs=placed,
        out_specs=(P(None, None, "gy", "gx"), P(None, ("gx", "gy"))),
        check_vma=False,
    )
```

```python
import functools

import jax
import jax.numpy as jnp
from jax import lax
from jax.experimental import pallas as pl
from jax.experimental.pallas import tpu as pltpu
from jax.sharding import PartitionSpec as P

A_DEV = 6912
HI = 27
PER = 4

def lanes_of(shape):
    return lax.broadcasted_iota(jnp.int32, shape, len(shape) - 1)

def wide(x, y=None):
    return jnp.concatenate([x, x if y is None else y], axis=1)

def strips_kernel(tracers, u_face, land_mask, to_east, to_west):
    lane = lanes_of((8, 128))
    spot = lane & 3
    east = jnp.zeros((8, 128), jnp.float32)
    west = jnp.zeros((8, 128), jnp.float32)
    wet = wide(land_mask[...].astype(jnp.float32))
    for p in range(32):
        here = lane >> 2 == p
        cells = wide(tracers[p // 16, p % 16])
        east = jnp.where(here, pltpu.roll(cells, (4 * p - 61) % 128, 1), east)
        west = jnp.where(here, pltpu.roll(cells, 4 * p, 1), west)
        last = 4 * p + 3
        if p < 16:
            east = jnp.where(lane == last, pltpu.roll(wide(u_face[p]), (last - 63) % 128, 1), east)
        elif p == 16:
            east = jnp.where(lane == last, pltpu.roll(wet, (last - 63) % 128, 1), east)
            west = jnp.where(lane == last, pltpu.roll(wet, last, 1), west)
    to_east[...] = east
    to_west[...] = west

def sweep(q, c, size, axis):
    def at(x, s):
        return pltpu.roll(x, (-s) % size, axis)
    nxt = at(q, 1)
    edge = (7.0 * (q + nxt) - (at(q, -1) + at(nxt, 1))) * (1.0 / 12.0)
    left = at(edge, -1)
    slope = edge - left
    curve = 6.0 * q - 3.0 * (left + edge)
    east = c >= 0.0
    size_c = jnp.abs(c)
    first = jnp.where(east, -slope, at(slope, 1))
    second = jnp.where(east, curve, at(curve, 1))
    flux = c * (edge + (0.5 * size_c) * (first + (1.0 - size_c * (2.0 / 3.0)) * second))
    return q - (flux - at(flux, -1))

def east_kernel(tracers, u_face, v_face, land_mask, from_west, from_east, swept, to_next, to_prev):
    lane = lanes_of((8, 128))
    own = lane < 64
    west_part = lane >= 96
    west = from_west[...]
    east = from_east[...]
    def put(cells, src, at_lane, lane_here, base):
        return jnp.where(lane == lane_here, pltpu.roll(src, (lane_here - at_lane) % 128, 1), base)
    wet = wide(land_mask[...].astype(jnp.float32))
    wet_x = put(None, west, 67, 127, put(None, east, 67, 64, wet))
    mm = wet_x * pltpu.roll(wet_x, 127, 1)
    for k in range(16):
        u = put(None, west, 4 * k + 3, 127, wide(u_face[k]))
        c = u * mm
        both = []
        for t in range(2):
            p = t * 16 + k
            halo = jnp.where(west_part, pltpu.roll(west, (125 - 4 * p) % 128, 1), pltpu.roll(east, (64 - 4 * p) % 128, 1))
            q = jnp.where(own, wide(tracers[t, k]), halo)
            both.append(sweep(q, c, 128, 1)[:, :64])
        z = wide(both[0], both[1])
        swept[k] = z
        to_next[k, 0:3, :] = z[5:8]
        to_prev[k, 0:3, :] = z[0:3]
        to_next[k, 3:4, :] = wide(v_face[k, 7:8, :], wet[7:8, :64])
        to_prev[k, 3:4, :] = wide(v_face[k, 0:1, :], wet[0:1, :64])

def north_kernel(swept, v_face, land_mask, thickness, from_prev, from_next, out):
    row = lax.broadcasted_iota(jnp.int32, (8, 128), 0)
    lane = lanes_of((8, 128))
    wet = wide(land_mask[...].astype(jnp.float32))
    def twin(x):
        return jnp.where(lane < 64, pltpu.roll(x, 64, 1), x)
    def eight(ref, k):
        x = ref[k]
        return jnp.concatenate([x, x], axis=0)
    prev0 = twin(eight(from_prev, 0)); next0 = twin(eight(from_next, 0))
    wet_y = jnp.concatenate([wet, jnp.where(row == 0, pltpu.roll(next0, (0 - 3) % 8, 0), prev0)], axis=0)
    mm = wet_y * pltpu.roll(wet_y, 15, 0)
    def flip(x):
        return jnp.where(lane < 64, x, pltpu.roll(x, 64, 1))
    z = []
    for k in range(16):
        prev = eight(from_prev, k)
        nxt = eight(from_next, k)
        v = jnp.concatenate([wide(v_face[k]), flip(prev)], axis=0)
        q = jnp.concatenate([swept[k], jnp.where(row < 4, nxt, pltpu.roll(prev, 1, 0))], axis=0)
        z.append(sweep(q, v * mm, 16, 0)[:8])
    tops = [jnp.zeros((8, 128), jnp.float32)]
    for j in range(16):
        tops.append(tops[-1] + wide(thickness[j]))
    thick = tops[16] * (1.0 / 16.0)
    inverse = 1.0 / thick
    for k in range(16):
        top = thick * float(k)
        base = thick * float(k + 1)
        total = jnp.zeros((8, 128), jnp.float32)
        for j in range(16):
            depth = jnp.maximum(jnp.minimum(tops[j + 1], base) - jnp.maximum(tops[j], top), 0.0)
            total = total + depth * z[j]
        total = total * inverse
        out[0, k] = total[:, :64]
        out[1, k] = total[:, 64:]

VM = pl.BlockSpec(memory_space=pltpu.VMEM)
def f32(*shape):
    return jax.ShapeDtypeStruct(shape, jnp.float32)
def call(kernel, name, outs, args):
    return pl.pallas_call(kernel, in_specs=[VM] * len(args), out_specs=[VM] * len(outs), out_shape=list(outs), compiler_params=pltpu.CompilerParams(vmem_limit_bytes=8 * 2**20), name=name)(*args)

def shift(x, axis, step):
    n = lax.axis_size(axis)
    pairs = [(i, i + 1) for i in range(n - 1)]
    if step < 0:
        pairs = [(j, i) for i, j in pairs]
    return lax.ppermute(x, axis, pairs)

def strips(tracers, u_face, land_mask):
    return call(strips_kernel, "column_strips", [f32(8, 128)] * 2, (tracers, u_face, land_mask))


def longitude(tracers, u_face, v_face, land_mask, from_west, from_east):
    return call(
        east_kernel,
        "sweep_longitude",
        [f32(16, 8, 128), f32(16, 4, 128), f32(16, 4, 128)],
        (tracers, u_face, v_face, land_mask, from_west, from_east),
    )


def latitude(swept, v_face, land_mask, thickness, from_prev, from_next):
    args = (swept, v_face, land_mask, thickness, from_prev, from_next)
    return call(north_kernel, "sweep_latitude", [f32(2, 16, 8, 64)], args)[0]


def lane_take(table, lanes):
    return jnp.take_along_axis(table, lanes, axis=1, mode="promise_in_bounds")
def gather_kernel(tracers, u_face, v_face, land_mask, counts, ocean_cell, weight, payload):
    def packed(x):
        return jnp.concatenate([x[0:4, :], x[4:8, :]], axis=1)
    wet = packed(land_mask[...].astype(jnp.float32))
    east = packed(u_face[0]); north = packed(v_face[0])
    speed = jnp.sqrt(east * east + north * north + 0.01) * wet
    fields = [packed(tracers[0, 0]) * speed, packed(tracers[1, 0]) * speed, east * speed, north * speed, wet]
    tables = [[jnp.broadcast_to(f[q:q+1, :], (8, 128)) for q in range(4)] for f in fields]
    used = jnp.broadcast_to(counts[...], (8, 128))
    sub = lax.broadcasted_iota(jnp.int32, (8, 128), 0)
    lane_ids = lax.broadcasted_iota(jnp.int32, (8, 128), 1)
    def step(g, _):
        o = pl.multiple_of(g * 8, 8)
        count = lane_take(used, sub + o)
        for h in range(2):
            cell = ocean_cell[0, pl.ds(o, 8), h*128:(h+1)*128]
            share = jnp.where(lane_ids + h*128 < count, weight[0, pl.ds(o, 8), h*128:(h+1)*128], 0.0)
            lanes = (cell & 63) | ((cell >> 2) & 64)
            odd = (cell & 64) != 0
            upper = (cell & 128) != 0
            for f in range(5):
                a, b, c, d = [lane_take(t, lanes) for t in tables[f]]
                val = jnp.where(upper, jnp.where(odd, d, c), jnp.where(odd, b, a))
                payload[pl.ds(g * 80 + f*2+h, 8, stride=10), :] = val * share
        return 0
    lax.fori_loop(0, 16, step, 0, unroll=16)


def scatter_kernel(received, atm_cell, flux, fin):
    sub = lax.broadcasted_iota(jnp.int32, (16, 128), 0)
    def bf(x):
        return x.astype(jnp.float32).astype(jnp.bfloat16)
    low_ids = [bf(sub + 16 * k) for k in range(16)]
    high_ids = []
    for k in range(17):
        first = (16 * k) // HI
        row = sub + 16 * k - first * HI
        row = jnp.where(row >= HI, row - HI, row)
        if k == 16:
            row = jnp.where(sub < 14, row, -1)
        high_ids.append(bf(row))
    one, zero = jnp.bfloat16(1), jnp.bfloat16(0)
    def spread(row):
        return jnp.broadcast_to(row, (16, 128)).astype(jnp.bfloat16)
    def run(*accs):
        accs = [accs[:17], accs[17:]]
        for m in range(2):
            for a in accs[m]:
                pltpu.matmul_pop(a)
        def chunk(cells, pieces, s, mxu, stage):
            low = [spread((c[s:s+1] & 255).astype(jnp.float32)) for c in cells]
            rhs = jnp.concatenate([jnp.concatenate([jnp.where(lo == ids, one, zero) for lo in low], axis=1) for ids in low_ids], axis=0)
            pltpu.matmul_push_rhs(rhs, stage, mxu, transpose=True)
            high = [spread((c[s:s+1] >> 8).astype(jnp.float32)) for c in cells]
            tiles = {}
            for k in range(17):
                first = (16 * k) // HI
                edge = (first + 1) * HI - 16 * k
                for j in (first, first + 1):
                    if j < 10 and j not in tiles:
                        tiles[j] = [spread(p[s:s+1]) for p in pieces[j]]
                halves = []
                for h in range(2):
                    v = tiles[first][h]
                    if edge < 16 and first + 1 < 10:
                        v = jnp.where(sub < edge, v, tiles[first + 1][h])
                    halves.append(jnp.where(high[h] == high_ids[k], v, zero))
                pltpu.matmul_acc_lhs(accs[mxu][k], jnp.concatenate(halves, axis=1), load_staged_rhs=stage if k == 0 else None)
        def step(i, _):
            for k in range(PER):
                g = i * PER + k
                cells = [atm_cell[0, pl.ds(pl.multiple_of(g * 8, 8), 8), h*128:h*128+128] for h in range(2)]
                pieces = []
                for f in range(5):
                    val = [received[pl.ds(g * 80 + f*2+h, 8, stride=10), :] for h in range(2)]
                    top = [v.astype(jnp.bfloat16).astype(jnp.float32) for v in val]
                    pieces += [top, [v - t for v, t in zip(val, top)]]
                for s in range(8):
                    chunk(cells, pieces, s, s % 2, (s // 2) % 2)
            return 0
        lax.fori_loop(0, 16 // PER, step, 0)
        for k in range(17):
            total = pltpu.matmul_pop(accs[0][k]) + pltpu.matmul_pop(accs[1][k])
            for half in range(2):
                fin[half*272+k*16:half*272+k*16+16, :] = total[:, half*128:half*128+128]
    pl.run_scoped(run, *([pltpu.ACC(0)((16, 256), jnp.float32)] * 17 + [pltpu.ACC(1)((16, 256), jnp.float32)] * 17))
    for hi in range(27):
        for half in range(2):
            b = half * 272 + hi
            num = fin[pl.ds(b, 4, stride=54), :] + fin[pl.ds(b+27, 4, stride=54), :]
            den = fin[b+216:b+217, :] + fin[b+243:b+244, :]
            flux[:, hi*256+half*128:hi*256+half*128+128] = num / jnp.maximum(den, 0.2)


def gather(tracers, u_face, v_face, land_mask, counts, ocean_cell, weight):
    return pl.pallas_call(
        gather_kernel,
        grid=(1,),
        in_specs=[
            pl.BlockSpec((2, 1, 8, 64), lambda i: (0, 0, 0, 0)),
            pl.BlockSpec((1, 8, 64), lambda i: (0, 0, 0)),
            pl.BlockSpec((1, 8, 64), lambda i: (0, 0, 0)),
            pl.BlockSpec((8, 64), lambda i: (0, 0)),
            pl.BlockSpec((1, 128), lambda i: (0, 0)),
            pl.BlockSpec((1, 128, 256), lambda i: (0, 0, 0)),
            pl.BlockSpec((1, 128, 256), lambda i: (0, 0, 0)),
        ],
        out_specs=pl.BlockSpec((1280, 128), lambda i: (0, 0)),
        out_shape=f32(1280, 128),
        name="weighted_slots",
    )(tracers, u_face, v_face, land_mask, counts, ocean_cell, weight)


def scatter(received, atm_cell):
    return pl.pallas_call(
        scatter_kernel,
        in_specs=[VM] * 2,
        out_specs=VM,
        out_shape=f32(4, A_DEV),
        scratch_shapes=[pltpu.VMEM((544, 128), jnp.float32)],
        compiler_params=pltpu.CompilerParams(vmem_limit_bytes=16 * 2**20),
        name="owner_sums",
    )(received, atm_cell)


def on_device(tracers, u_face, v_face, thickness, land_mask, counts, ocean_cell, xgrid_weight, atm_cell):
    payload = gather(tracers, u_face, v_face, land_mask, counts, ocean_cell, xgrid_weight)
    received = lax.all_to_all(payload.reshape(128, 1, 1280), ("gx", "gy"), split_axis=0, concat_axis=0, tiled=True)
    to_east, to_west = strips(tracers, u_face, land_mask)
    from_west = shift(to_east, "gx", 1)
    from_east = shift(to_west, "gx", -1)
    swept, to_next, to_prev = longitude(tracers, u_face, v_face, land_mask, from_west, from_east)
    received, _ = lax.optimization_barrier((received, to_next))
    from_prev = shift(to_next, "gy", 1)
    from_next = shift(to_prev, "gy", -1)
    atm_flux = scatter(received.reshape(1280, 128), atm_cell)
    atm_flux, from_prev, from_next = lax.optimization_barrier((atm_flux, from_prev, from_next))
    tracers_new = latitude(swept, v_face, land_mask, thickness, from_prev, from_next)
    return (tracers_new, atm_flux)


def solution(mesh):
    placed = (
        P(None, None, "gy", "gx"),
        P(None, "gy", "gx"),
        P(None, "gy", "gx"),
        P(None, "gy", "gx"),
        P("gy", "gx"),
        P(("gx", "gy"), None),
        P(("gx", "gy"), None, None),
        P(("gx", "gy"), None, None),
        P(("gx", "gy"), None, None),
    )
    return jax.shard_map(
        on_device,
        mesh=mesh,
        in_specs=placed,
        out_specs=(P(None, None, "gy", "gx"), P(None, ("gx", "gy"))),
        check_vma=False,
    )
```

```python
import functools

import jax
import jax.numpy as jnp
from jax import lax
from jax.experimental import pallas as pl
from jax.experimental.pallas import tpu as pltpu
from jax.sharding import PartitionSpec as P

A_DEV = 6912
HI = 27
PER = 8

def lanes_of(shape):
    return lax.broadcasted_iota(jnp.int32, shape, len(shape) - 1)

def wide(x, y=None):
    return jnp.concatenate([x, x if y is None else y], axis=1)

def even_index(axis):
    return lax.rem(lax.axis_index(axis), 2) == 0


def strips_kernel(tracers, u_face, land_mask, to_near, to_far):
    lane = lanes_of((8, 128))
    spot = lane & 3
    east = jnp.zeros((8, 128), jnp.float32)
    west = jnp.zeros((8, 128), jnp.float32)
    wet = wide(land_mask[...].astype(jnp.float32))
    for p in range(32):
        here = lane >> 2 == p
        cells = wide(tracers[p // 16, p % 16])
        east = jnp.where(here, pltpu.roll(cells, (4 * p - 61) % 128, 1), east)
        west = jnp.where(here, pltpu.roll(cells, 4 * p, 1), west)
        last = 4 * p + 3
        if p < 16:
            east = jnp.where(lane == last, pltpu.roll(wide(u_face[p]), (last - 63) % 128, 1), east)
        elif p == 16:
            east = jnp.where(lane == last, pltpu.roll(wet, (last - 63) % 128, 1), east)
            west = jnp.where(lane == last, pltpu.roll(wet, last, 1), west)
    even = even_index("gx")
    to_near[...] = jnp.where(even, east, west)
    to_far[...] = jnp.where(even, west, east)

def sweep(q, c, size, axis):
    def at(x, s):
        return pltpu.roll(x, (-s) % size, axis)
    nxt = at(q, 1)
    edge = (7.0 * (q + nxt) - (at(q, -1) + at(nxt, 1))) * (1.0 / 12.0)
    left = at(edge, -1)
    slope = edge - left
    curve = 6.0 * q - 3.0 * (left + edge)
    east = c >= 0.0
    size_c = jnp.abs(c)
    first = jnp.where(east, -slope, at(slope, 1))
    second = jnp.where(east, curve, at(curve, 1))
    flux = c * (edge + (0.5 * size_c) * (first + (1.0 - size_c * (2.0 / 3.0)) * second))
    return q - (flux - at(flux, -1))

def east_kernel(tracers, u_face, v_face, land_mask, from_near, from_far, swept, to_pair, to_other):
    even_row = even_index("gy")
    lane = lanes_of((8, 128))
    own = lane < 64
    west_part = lane >= 96
    even = even_index("gx")
    west = jnp.where(even, from_far[...], from_near[...])
    east = jnp.where(even, from_near[...], from_far[...])
    def put(cells, src, at_lane, lane_here, base):
        return jnp.where(lane == lane_here, pltpu.roll(src, (lane_here - at_lane) % 128, 1), base)
    wet = wide(land_mask[...].astype(jnp.float32))
    wet_x = put(None, west, 67, 127, put(None, east, 67, 64, wet))
    mm = wet_x * pltpu.roll(wet_x, 127, 1)
    for k in range(16):
        u = put(None, west, 4 * k + 3, 127, wide(u_face[k]))
        c = u * mm
        both = []
        for t in range(2):
            p = t * 16 + k
            halo = jnp.where(west_part, pltpu.roll(west, (125 - 4 * p) % 128, 1), pltpu.roll(east, (64 - 4 * p) % 128, 1))
            q = jnp.where(own, wide(tracers[t, k]), halo)
            both.append(sweep(q, c, 128, 1)[:, :64])
        z = wide(both[0], both[1])
        swept[k] = z
        last = (z[5:8], wide(v_face[k, 7:8, :], wet[7:8, :64]))
        first = (z[0:3], wide(v_face[k, 0:1, :], wet[0:1, :64]))
        for rows, a, b in ((slice(0, 3), last[0], first[0]), (slice(3, 4), last[1], first[1])):
            to_pair[k, rows, :] = jnp.where(even_row, a, b)
            to_other[k, rows, :] = jnp.where(even_row, b, a)


def north_kernel(swept, v_face, land_mask, thickness, from_pair, from_other, out):
    even_row = even_index("gy")
    row = lax.broadcasted_iota(jnp.int32, (8, 128), 0)
    lane = lanes_of((8, 128))
    wet = wide(land_mask[...].astype(jnp.float32))
    def twin(x):
        return jnp.where(lane < 64, pltpu.roll(x, 64, 1), x)
    def halos(k):
        pair, other = from_pair[k], from_other[k]
        prev, nxt = jnp.where(even_row, other, pair), jnp.where(even_row, pair, other)
        return jnp.concatenate([prev, prev], axis=0), jnp.concatenate([nxt, nxt], axis=0)

    prev0, next0 = [twin(x) for x in halos(0)]
    wet_y = jnp.concatenate([wet, jnp.where(row == 0, pltpu.roll(next0, (0 - 3) % 8, 0), prev0)], axis=0)
    mm = wet_y * pltpu.roll(wet_y, 15, 0)
    def flip(x):
        return jnp.where(lane < 64, x, pltpu.roll(x, 64, 1))
    z = []
    for k in range(16):
        prev, nxt = halos(k)
        v = jnp.concatenate([wide(v_face[k]), flip(prev)], axis=0)
        q = jnp.concatenate([swept[k], jnp.where(row < 4, nxt, pltpu.roll(prev, 1, 0))], axis=0)
        z.append(sweep(q, v * mm, 16, 0)[:8])
    tops = [jnp.zeros((8, 128), jnp.float32)]
    for j in range(16):
        tops.append(tops[-1] + wide(thickness[j]))
    thick = tops[16] * (1.0 / 16.0)
    inverse = 1.0 / thick
    for k in range(16):
        top = thick * float(k)
        base = thick * float(k + 1)
        total = jnp.zeros((8, 128), jnp.float32)
        for j in range(16):
            depth = jnp.maximum(jnp.minimum(tops[j + 1], base) - jnp.maximum(tops[j], top), 0.0)
            total = total + depth * z[j]
        total = total * inverse
        out[0, k] = total[:, :64]
        out[1, k] = total[:, 64:]

VM = pl.BlockSpec(memory_space=pltpu.VMEM)
def f32(*shape):
    return jax.ShapeDtypeStruct(shape, jnp.float32)
def call(kernel, name, outs, args):
    return pl.pallas_call(kernel, in_specs=[VM] * len(args), out_specs=[VM] * len(outs), out_shape=list(outs), compiler_params=pltpu.CompilerParams(vmem_limit_bytes=8 * 2**20), name=name)(*args)

def swap(x, axis, first):
    n = lax.axis_size(axis)
    pairs = [(i, i + 1) for i in range(first, n - 1, 2)]
    return lax.ppermute(x, axis, pairs + [(j, i) for i, j in pairs])


def strips(tracers, u_face, land_mask):
    return call(strips_kernel, "column_strips", [f32(8, 128)] * 2, (tracers, u_face, land_mask))


def longitude(tracers, u_face, v_face, land_mask, from_near, from_far):
    return call(
        east_kernel,
        "sweep_longitude",
        [f32(16, 8, 128), f32(16, 4, 128), f32(16, 4, 128)],
        (tracers, u_face, v_face, land_mask, from_near, from_far),
    )


def latitude(swept, v_face, land_mask, thickness, from_pair, from_other):
    args = (swept, v_face, land_mask, thickness, from_pair, from_other)
    return call(north_kernel, "sweep_latitude", [f32(2, 16, 8, 64)], args)[0]


def lane_take(table, lanes):
    return jnp.take_along_axis(table, lanes, axis=1, mode="promise_in_bounds")
def gather_kernel(tracers, u_face, v_face, land_mask, counts, ocean_cell, weight, payload):
    def packed(x):
        return jnp.concatenate([x[0:4, :], x[4:8, :]], axis=1)
    wet = packed(land_mask[...].astype(jnp.float32))
    east = packed(u_face[0]); north = packed(v_face[0])
    speed = jnp.sqrt(east * east + north * north + 0.01) * wet
    fields = [packed(tracers[0, 0]) * speed, packed(tracers[1, 0]) * speed, east * speed, north * speed, wet]
    tables = [[jnp.broadcast_to(f[q:q+1, :], (8, 128)) for q in range(4)] for f in fields]
    used = jnp.broadcast_to(counts[...], (8, 128))
    sub = lax.broadcasted_iota(jnp.int32, (8, 128), 0)
    lane_ids = lax.broadcasted_iota(jnp.int32, (8, 128), 1)
    def step(g, _):
        o = pl.multiple_of(g * 8, 8)
        count = lane_take(used, sub + o)
        for h in range(2):
            cell = ocean_cell[0, pl.ds(o, 8), h*128:(h+1)*128]
            share = jnp.where(lane_ids + h*128 < count, weight[0, pl.ds(o, 8), h*128:(h+1)*128], 0.0)
            lanes = (cell & 63) | ((cell >> 2) & 64)
            odd = (cell & 64) != 0
            upper = (cell & 128) != 0
            for f in range(5):
                a, b, c, d = [lane_take(t, lanes) for t in tables[f]]
                val = jnp.where(upper, jnp.where(odd, d, c), jnp.where(odd, b, a))
                payload[pl.ds(g * 80 + f*2+h, 8, stride=10), :] = val * share
        return 0
    lax.fori_loop(0, 16, step, 0, unroll=16)


def scatter_kernel(received, atm_cell, flux, fin):
    sub = lax.broadcasted_iota(jnp.int32, (16, 128), 0)
    def bf(x):
        return x.astype(jnp.float32).astype(jnp.bfloat16)
    low_ids = [bf(sub + 16 * k) for k in range(16)]
    high_ids = []
    for k in range(17):
        first = (16 * k) // HI
        row = sub + 16 * k - first * HI
        row = jnp.where(row >= HI, row - HI, row)
        if k == 16:
            row = jnp.where(sub < 14, row, -1)
        high_ids.append(bf(row))
    one, zero = jnp.bfloat16(1), jnp.bfloat16(0)
    def spread(row):
        return jnp.broadcast_to(row, (16, 128)).astype(jnp.bfloat16)
    def run(*accs):
        accs = [accs[:17], accs[17:]]
        for m in range(2):
            for a in accs[m]:
                pltpu.matmul_pop(a)
        def chunk(cells, pieces, s, mxu, stage):
            low = [spread((c[s:s+1] & 255).astype(jnp.float32)) for c in cells]
            rhs = jnp.concatenate([jnp.concatenate([jnp.where(lo == ids, one, zero) for lo in low], axis=1) for ids in low_ids], axis=0)
            pltpu.matmul_push_rhs(rhs, stage, mxu, transpose=True)
            high = [spread((c[s:s+1] >> 8).astype(jnp.float32)) for c in cells]
            tiles = {}
            for k in range(17):
                first = (16 * k) // HI
                edge = (first + 1) * HI - 16 * k
                for j in (first, first + 1):
                    if j < 10 and j not in tiles:
                        tiles[j] = [spread(p[s:s+1]) for p in pieces[j]]
                halves = []
                for h in range(2):
                    v = tiles[first][h]
                    if edge < 16 and first + 1 < 10:
                        v = jnp.where(sub < edge, v, tiles[first + 1][h])
                    halves.append(jnp.where(high[h] == high_ids[k], v, zero))
                pltpu.matmul_acc_lhs(accs[mxu][k], jnp.concatenate(halves, axis=1), load_staged_rhs=stage if k == 0 else None)
        def step(i, _):
            for k in range(PER):
                g = i * PER + k
                cells = [atm_cell[0, pl.ds(pl.multiple_of(g * 8, 8), 8), h*128:h*128+128] for h in range(2)]
                pieces = []
                for f in range(5):
                    val = [received[pl.ds(g * 80 + f*2+h, 8, stride=10), :] for h in range(2)]
                    top = [v.astype(jnp.bfloat16).astype(jnp.float32) for v in val]
                    pieces += [top, [v - t for v, t in zip(val, top)]]
                for s in range(8):
                    chunk(cells, pieces, s, s % 2, (s // 2) % 2)
            return 0
        lax.fori_loop(0, 16 // PER, step, 0)
        for k in range(17):
            total = pltpu.matmul_pop(accs[0][k]) + pltpu.matmul_pop(accs[1][k])
            for half in range(2):
                fin[half*272+k*16:half*272+k*16+16, :] = total[:, half*128:half*128+128]
    pl.run_scoped(run, *([pltpu.ACC(0)((16, 256), jnp.float32)] * 17 + [pltpu.ACC(1)((16, 256), jnp.float32)] * 17))
    for hi in range(27):
        for half in range(2):
            b = half * 272 + hi
            num = fin[pl.ds(b, 4, stride=54), :] + fin[pl.ds(b+27, 4, stride=54), :]
            den = fin[b+216:b+217, :] + fin[b+243:b+244, :]
            flux[:, hi*256+half*128:hi*256+half*128+128] = num / jnp.maximum(den, 0.2)


def gather(tracers, u_face, v_face, land_mask, counts, ocean_cell, weight):
    return pl.pallas_call(
        gather_kernel,
        grid=(1,),
        in_specs=[
            pl.BlockSpec((2, 1, 8, 64), lambda i: (0, 0, 0, 0)),
            pl.BlockSpec((1, 8, 64), lambda i: (0, 0, 0)),
            pl.BlockSpec((1, 8, 64), lambda i: (0, 0, 0)),
            pl.BlockSpec((8, 64), lambda i: (0, 0)),
            pl.BlockSpec((1, 128), lambda i: (0, 0)),
            pl.BlockSpec((1, 128, 256), lambda i: (0, 0, 0)),
            pl.BlockSpec((1, 128, 256), lambda i: (0, 0, 0)),
        ],
        out_specs=pl.BlockSpec((1280, 128), lambda i: (0, 0)),
        out_shape=f32(1280, 128),
        name="weighted_slots",
    )(tracers, u_face, v_face, land_mask, counts, ocean_cell, weight)


def scatter(received, atm_cell):
    return pl.pallas_call(
        scatter_kernel,
        in_specs=[VM] * 2,
        out_specs=VM,
        out_shape=f32(4, A_DEV),
        scratch_shapes=[pltpu.VMEM((544, 128), jnp.float32)],
        compiler_params=pltpu.CompilerParams(vmem_limit_bytes=16 * 2**20),
        name="owner_sums",
    )(received, atm_cell)


def on_device(tracers, u_face, v_face, thickness, land_mask, counts, ocean_cell, xgrid_weight, atm_cell):
    payload = gather(tracers, u_face, v_face, land_mask, counts, ocean_cell, xgrid_weight)
    received = lax.all_to_all(payload.reshape(128, 1, 1280), ("gx", "gy"), split_axis=0, concat_axis=0, tiled=True)
    to_near, to_far = strips(tracers, u_face, land_mask)
    from_far = swap(to_far, "gx", 1)
    from_near = swap(to_near, "gx", 0)
    swept, to_pair, to_other = longitude(tracers, u_face, v_face, land_mask, from_near, from_far)
    received, _ = lax.optimization_barrier((received, to_pair))
    from_other = swap(to_other, "gy", 1)
    from_pair = swap(to_pair, "gy", 0)
    atm_flux = scatter(received.reshape(1280, 128), atm_cell)
    atm_flux, from_pair, from_other = lax.optimization_barrier((atm_flux, from_pair, from_other))
    tracers_new = latitude(swept, v_face, land_mask, thickness, from_pair, from_other)
    return (tracers_new, atm_flux)


def solution(mesh):
    placed = (
        P(None, None, "gy", "gx"),
        P(None, "gy", "gx"),
        P(None, "gy", "gx"),
        P(None, "gy", "gx"),
        P("gy", "gx"),
        P(("gx", "gy"), None),
        P(("gx", "gy"), None, None),
        P(("gx", "gy"), None, None),
        P(("gx", "gy"), None, None),
    )
    return jax.shard_map(
        on_device,
        mesh=mesh,
        in_specs=placed,
        out_specs=(P(None, None, "gy", "gx"), P(None, ("gx", "gy"))),
        check_vma=False,
    )
```

```python
import jax
import jax.numpy as jnp
from jax import lax
from jax.experimental import pallas as pl
from jax.experimental.pallas import tpu as pltpu
from jax.sharding import PartitionSpec as P

A_DEV = 6912
PIECES = 3
PER = 8
F8 = jnp.float8_e4m3fn


def lanes_of(shape):
    return lax.broadcasted_iota(jnp.int32, shape, len(shape) - 1)

def wide(x, y=None):
    return jnp.concatenate([x, x if y is None else y], axis=1)

def even_index(axis):
    return lax.rem(lax.axis_index(axis), 2) == 0


def strips_kernel(tracers, u_face, land_mask, to_near, to_far):
    lane = lanes_of((8, 128))
    spot = lane & 3
    east = jnp.zeros((8, 128), jnp.float32)
    west = jnp.zeros((8, 128), jnp.float32)
    wet = wide(land_mask[...].astype(jnp.float32))
    for p in range(32):
        here = lane >> 2 == p
        cells = wide(tracers[p // 16, p % 16])
        east = jnp.where(here, pltpu.roll(cells, (4 * p - 61) % 128, 1), east)
        west = jnp.where(here, pltpu.roll(cells, 4 * p, 1), west)
        last = 4 * p + 3
        if p < 16:
            east = jnp.where(lane == last, pltpu.roll(wide(u_face[p]), (last - 63) % 128, 1), east)
        elif p == 16:
            east = jnp.where(lane == last, pltpu.roll(wet, (last - 63) % 128, 1), east)
            west = jnp.where(lane == last, pltpu.roll(wet, last, 1), west)
    even = even_index("gx")
    to_near[...] = jnp.where(even, east, west)
    to_far[...] = jnp.where(even, west, east)

def sweep(q, c, size, axis):
    def at(x, s):
        return pltpu.roll(x, (-s) % size, axis)
    nxt = at(q, 1)
    edge = (7.0 * (q + nxt) - (at(q, -1) + at(nxt, 1))) * (1.0 / 12.0)
    left = at(edge, -1)
    slope = edge - left
    curve = 6.0 * q - 3.0 * (left + edge)
    east = c >= 0.0
    size_c = jnp.abs(c)
    first = jnp.where(east, -slope, at(slope, 1))
    second = jnp.where(east, curve, at(curve, 1))
    flux = c * (edge + (0.5 * size_c) * (first + (1.0 - size_c * (2.0 / 3.0)) * second))
    return q - (flux - at(flux, -1))

def east_kernel(tracers, u_face, v_face, land_mask, from_near, from_far, swept, to_pair, to_other):
    even_row = even_index("gy")
    lane = lanes_of((8, 128))
    own = lane < 64
    west_part = lane >= 96
    even = even_index("gx")
    west = jnp.where(even, from_far[...], from_near[...])
    east = jnp.where(even, from_near[...], from_far[...])
    def put(cells, src, at_lane, lane_here, base):
        return jnp.where(lane == lane_here, pltpu.roll(src, (lane_here - at_lane) % 128, 1), base)
    wet = wide(land_mask[...].astype(jnp.float32))
    wet_x = put(None, west, 67, 127, put(None, east, 67, 64, wet))
    mm = wet_x * pltpu.roll(wet_x, 127, 1)
    for k in range(16):
        u = put(None, west, 4 * k + 3, 127, wide(u_face[k]))
        c = u * mm
        both = []
        for t in range(2):
            p = t * 16 + k
            halo = jnp.where(west_part, pltpu.roll(west, (125 - 4 * p) % 128, 1), pltpu.roll(east, (64 - 4 * p) % 128, 1))
            q = jnp.where(own, wide(tracers[t, k]), halo)
            both.append(sweep(q, c, 128, 1)[:, :64])
        z = wide(both[0], both[1])
        swept[k] = z
        last = (z[5:8], wide(v_face[k, 7:8, :], wet[7:8, :64]))
        first = (z[0:3], wide(v_face[k, 0:1, :], wet[0:1, :64]))
        for rows, a, b in ((slice(0, 3), last[0], first[0]), (slice(3, 4), last[1], first[1])):
            to_pair[k, rows, :] = jnp.where(even_row, a, b)
            to_other[k, rows, :] = jnp.where(even_row, b, a)


def north_kernel(swept, v_face, land_mask, thickness, from_pair, from_other, out):
    even_row = even_index("gy")
    row = lax.broadcasted_iota(jnp.int32, (8, 128), 0)
    lane = lanes_of((8, 128))
    wet = wide(land_mask[...].astype(jnp.float32))
    def twin(x):
        return jnp.where(lane < 64, pltpu.roll(x, 64, 1), x)
    def halos(k):
        pair, other = from_pair[k], from_other[k]
        prev, nxt = jnp.where(even_row, other, pair), jnp.where(even_row, pair, other)
        return jnp.concatenate([prev, prev], axis=0), jnp.concatenate([nxt, nxt], axis=0)

    prev0, next0 = [twin(x) for x in halos(0)]
    wet_y = jnp.concatenate([wet, jnp.where(row == 0, pltpu.roll(next0, (0 - 3) % 8, 0), prev0)], axis=0)
    mm = wet_y * pltpu.roll(wet_y, 15, 0)
    def flip(x):
        return jnp.where(lane < 64, x, pltpu.roll(x, 64, 1))
    z = []
    for k in range(16):
        prev, nxt = halos(k)
        v = jnp.concatenate([wide(v_face[k]), flip(prev)], axis=0)
        q = jnp.concatenate([swept[k], jnp.where(row < 4, nxt, pltpu.roll(prev, 1, 0))], axis=0)
        z.append(sweep(q, v * mm, 16, 0)[:8])
    tops = [jnp.zeros((8, 128), jnp.float32)]
    for j in range(16):
        tops.append(tops[-1] + wide(thickness[j]))
    thick = tops[16] * (1.0 / 16.0)
    inverse = 1.0 / thick
    for k in range(16):
        top = thick * float(k)
        base = thick * float(k + 1)
        total = jnp.zeros((8, 128), jnp.float32)
        for j in range(16):
            depth = jnp.maximum(jnp.minimum(tops[j + 1], base) - jnp.maximum(tops[j], top), 0.0)
            total = total + depth * z[j]
        total = total * inverse
        out[0, k] = total[:, :64]
        out[1, k] = total[:, 64:]

VM = pl.BlockSpec(memory_space=pltpu.VMEM)
ANY = pl.BlockSpec(memory_space=pl.ANY)


def f32(*shape):
    return jax.ShapeDtypeStruct(shape, jnp.float32)
def call(kernel, name, outs, args):
    return pl.pallas_call(
        kernel,
        in_specs=[VM] * len(args),
        out_specs=[VM] * len(outs),
        out_shape=list(outs),
        compiler_params=pltpu.CompilerParams(vmem_limit_bytes=8 * 2**20),
        name=name,
    )(*args)


def swap(x, axis, first):
    n = lax.axis_size(axis)
    pairs = [(i, i + 1) for i in range(first, n - 1, 2)]
    return lax.ppermute(x, axis, pairs + [(j, i) for i, j in pairs])


def strips(tracers, u_face, land_mask):
    return call(strips_kernel, "column_strips", [f32(8, 128)] * 2, (tracers, u_face, land_mask))


def longitude(tracers, u_face, v_face, land_mask, from_near, from_far):
    return call(
        east_kernel,
        "sweep_longitude",
        [f32(16, 8, 128), f32(16, 4, 128), f32(16, 4, 128)],
        (tracers, u_face, v_face, land_mask, from_near, from_far),
    )


def latitude(swept, v_face, land_mask, thickness, from_pair, from_other):
    args = (swept, v_face, land_mask, thickness, from_pair, from_other)
    return call(north_kernel, "sweep_latitude", [f32(2, 16, 8, 64)], args)[0]


CHUNKS = 2


def lane_take(table, lanes):
    return jnp.take_along_axis(table, lanes, axis=1, mode="promise_in_bounds")


def gather_kernel(
    tracers, u_face, v_face, land_mask, counts, ocean_cell, weight, payload,
    heat, east_in, north_in, mask, used_in, cells, shares, staged, small_sem, cell_sem, share_sem, out_sem,
):
    owners = 128 // CHUNKS
    small = [
        (tracers.at[:, 0], heat), (u_face.at[0], east_in), (v_face.at[0], north_in), (land_mask, mask), (counts, used_in),
    ]
    small = [pltpu.make_async_copy(src, dst, small_sem.at[i]) for i, (src, dst) in enumerate(small)]
    for copy in small:
        copy.start()
    loads = []
    for i in range(CHUNKS):
        rows = pl.ds(i * owners, owners)
        loads.append((
            pltpu.make_async_copy(ocean_cell.at[0, rows], cells.at[rows], cell_sem.at[i]),
            pltpu.make_async_copy(weight.at[0, rows], shares.at[rows], share_sem.at[i]),
        ))
        for copy in loads[-1]:
            copy.start()
    for copy in small:
        copy.wait()

    def packed(x):
        return jnp.concatenate([x[0:4, :], x[4:8, :]], axis=1)

    wet = packed(mask[...].astype(jnp.float32))
    east = packed(east_in[...])
    north = packed(north_in[...])
    speed = jnp.sqrt(east * east + north * north + 0.01) * wet
    fields = [packed(heat[0]) * speed, packed(heat[1]) * speed, east * speed, north * speed, wet]
    tables = [[jnp.broadcast_to(f[q:q+1, :], (8, 128)) for q in range(4)] for f in fields]
    used = jnp.broadcast_to(used_in[...], (8, 128))
    sub = lax.broadcasted_iota(jnp.int32, (8, 128), 0)
    lane_ids = lax.broadcasted_iota(jnp.int32, (8, 128), 1)
    stores = []
    for i in range(CHUNKS):
        for copy in loads[i]:
            copy.wait()
        for g in range(i * owners // 8, (i + 1) * owners // 8):
            o = g * 8
            count = lane_take(used, sub + o)
            for h in range(2):
                part = slice(h * 128, (h + 1) * 128)
                cell = cells[o:o+8, part]
                share = jnp.where(lane_ids + h * 128 < count, shares[o:o+8, part], 0.0)
                lanes = (cell & 63) | ((cell >> 2) & 64)
                odd = (cell & 64) != 0
                upper = (cell & 128) != 0
                for f in range(5):
                    a, b, c, d = [lane_take(t, lanes) for t in tables[f]]
                    val = jnp.where(upper, jnp.where(odd, d, c), jnp.where(odd, b, a))
                    staged[pl.ds(g * 80 + f * 2 + h, 8, stride=10), :] = val * share
        rows = pl.ds(i * owners * 10, owners * 10)
        stores.append(pltpu.make_async_copy(staged.at[rows], payload.at[rows], out_sem.at[i]))
        stores[-1].start()
    for copy in stores:
        copy.wait()


def gather(tracers, u_face, v_face, land_mask, counts, ocean_cell, weight):
    return pl.pallas_call(
        gather_kernel,
        in_specs=[ANY] * 7,
        out_specs=ANY,
        out_shape=f32(1280, 128),
        scratch_shapes=[
            pltpu.VMEM((2, 8, 64), jnp.float32),
            pltpu.VMEM((8, 64), jnp.float32),
            pltpu.VMEM((8, 64), jnp.float32),
            pltpu.VMEM((8, 64), jnp.int32),
            pltpu.VMEM((1, 128), jnp.int32),
            pltpu.VMEM((128, 256), jnp.int32),
            pltpu.VMEM((128, 256), jnp.float32),
            pltpu.VMEM((1280, 128), jnp.float32),
            pltpu.SemaphoreType.DMA((5,)),
            pltpu.SemaphoreType.DMA((CHUNKS,)),
            pltpu.SemaphoreType.DMA((CHUNKS,)),
            pltpu.SemaphoreType.DMA((CHUNKS,)),
        ],
        name="weighted_slots",
    )(tracers, u_face, v_face, land_mask, counts, ocean_cell, weight)


def scatter_kernel(received, atm_cell, flux, fin):
    sub = lax.broadcasted_iota(jnp.int32, (16, 128), 0)
    def bf(x):
        return x.astype(jnp.float32).astype(jnp.bfloat16)
    ids = [bf(sub + 16 * k) for k in range(16)]
    zero8 = jnp.zeros((32, 128), F8)
    one8 = jnp.ones((32, 128), F8)
    def spread(row):
        return jnp.broadcast_to(row, (16, 128)).astype(jnp.bfloat16)
    peak = [jnp.zeros((8, 128), jnp.float32)] * 5
    for g in range(16):
        for f in range(5):
            for h in range(2):
                peak[f] = jnp.maximum(peak[f], jnp.abs(received[pl.ds(g * 80 + f*2+h, 8, stride=10), :]))
    scale = []
    back = []
    for f in range(5):
        top = jnp.maximum(jnp.max(jnp.max(peak[f], axis=0, keepdims=True), axis=1, keepdims=True), 1e-30)
        scale.append(jnp.broadcast_to(224.0 / top, (8, 128)))
        back.append(jnp.broadcast_to(top * (1.0 / 224.0), (8, 128)))
    def run(*accs):
        n = len(accs) // 2
        accs = [accs[:n], accs[n:]]
        for m in range(2):
            for a in accs[m]:
                pltpu.matmul_pop(a)
        def chunk(cells, pieces, s, mxu, stage):
            low = [spread((c[s:s+1] & 255).astype(jnp.float32)) for c in cells]
            high = [spread((c[s:s+1] >> 8).astype(jnp.float32)) for c in cells]
            cols = []
            for h in range(2):
                lo32 = jnp.concatenate([low[h], low[h]], axis=0)
                rows = [jnp.where(lo32 == jnp.concatenate([ids[2*k], ids[2*k+1]], axis=0), one8, zero8) for k in range(8)]
                cols.append(jnp.concatenate(rows, axis=0))
            pltpu.matmul_push_rhs(jnp.concatenate(cols, axis=1), stage, mxu, transpose=True)
            hit8 = [jnp.concatenate([x, x], axis=0) == jnp.concatenate([ids[0], ids[1]], axis=0) for x in high]
            for j in range(5 * PIECES):
                halves = []
                for h in range(2):
                    v = jnp.broadcast_to(pieces[j][h][s:s+1], (32, 128)).astype(F8)
                    halves.append(jnp.where(hit8[h], v, zero8))
                pltpu.matmul_acc_lhs(accs[mxu][j], jnp.concatenate(halves, axis=1), load_staged_rhs=stage if j == 0 else None)
        def step(i, _):
            for k in range(PER):
                g = i * PER + k
                cells = [atm_cell[0, pl.ds(pl.multiple_of(g * 8, 8), 8), h*128:h*128+128] for h in range(2)]
                pieces = []
                for f in range(5):
                    rest = [received[pl.ds(g * 80 + f*2+h, 8, stride=10), :] * scale[f] for h in range(2)]
                    for p in range(PIECES):
                        part = [r.astype(F8).astype(jnp.float32) for r in rest]
                        pieces.append(part)
                        rest = [(r - t) * 16.0 for r, t in zip(rest, part)]
                for s in range(8):
                    chunk(cells, pieces, s, s % 2, (s // 2) % 2)
            return 0
        lax.fori_loop(0, 16 // PER, step, 0)
        for f in range(5):
            total = 0.0
            for p in reversed(range(PIECES)):
                total = total * (1.0 / 16.0) + (pltpu.matmul_pop(accs[0][f*PIECES+p]) + pltpu.matmul_pop(accs[1][f*PIECES+p]))
            unit = jnp.concatenate([back[f]] * 4, axis=0)
            for half in range(2):
                fin[half*160+f*32:half*160+f*32+32, :] = total[:, half*128:half*128+128] * unit
    pl.run_scoped(run, *([pltpu.ACC(0)((32, 256), jnp.float32)] * (5*PIECES) + [pltpu.ACC(1)((32, 256), jnp.float32)] * (5*PIECES)))
    for hi in range(27):
        for half in range(2):
            b = half * 160 + hi
            num = fin[pl.ds(b, 4, stride=32), :]
            den = fin[b+128:b+129, :]
            flux[:, hi*256+half*128:hi*256+half*128+128] = num / jnp.maximum(den, 0.2)


def scatter(received, atm_cell):
    return pl.pallas_call(
        scatter_kernel,
        in_specs=[VM] * 2,
        out_specs=VM,
        out_shape=f32(4, A_DEV),
        scratch_shapes=[pltpu.VMEM((320, 128), jnp.float32)],
        compiler_params=pltpu.CompilerParams(vmem_limit_bytes=16 * 2**20),
        name="owner_sums",
    )(received, atm_cell)


def on_device(tracers, u_face, v_face, thickness, land_mask, counts, ocean_cell, xgrid_weight, atm_cell):
    payload = gather(tracers, u_face, v_face, land_mask, counts, ocean_cell, xgrid_weight)
    received = lax.all_to_all(payload.reshape(128, 1, 1280), ("gx", "gy"), split_axis=0, concat_axis=0, tiled=True)
    to_near, to_far = strips(tracers, u_face, land_mask)
    from_far = swap(to_far, "gx", 1)
    from_near = swap(to_near, "gx", 0)
    swept, to_pair, to_other = longitude(tracers, u_face, v_face, land_mask, from_near, from_far)
    received, _ = lax.optimization_barrier((received, to_pair))
    from_other = swap(to_other, "gy", 1)
    from_pair = swap(to_pair, "gy", 0)
    atm_flux = scatter(received.reshape(1280, 128), atm_cell)
    atm_flux, from_pair, from_other = lax.optimization_barrier((atm_flux, from_pair, from_other))
    tracers_new = latitude(swept, v_face, land_mask, thickness, from_pair, from_other)
    return (tracers_new, atm_flux)


def solution(mesh):
    placed = (
        P(None, None, "gy", "gx"),
        P(None, "gy", "gx"),
        P(None, "gy", "gx"),
        P(None, "gy", "gx"),
        P("gy", "gx"),
        P(("gx", "gy"), None),
        P(("gx", "gy"), None, None),
        P(("gx", "gy"), None, None),
        P(("gx", "gy"), None, None),
    )
    return jax.shard_map(
        on_device,
        mesh=mesh,
        in_specs=placed,
        out_specs=(P(None, None, "gy", "gx"), P(None, ("gx", "gy"))),
        check_vma=False,
    )
```
